512 devices in a mesh: gz: 32 (over x_lo, z, core), gx: 16 (over y, x_hi).
Axes of the slice: x: 4 (x_hi: 2, x_lo: 2; x = x_hi * 2 + x_lo), y: 8, z: 8, core: 2. Of those that a mesh axis runs over, the one named last changes fastest.
Arguments:
- image: bfloat16 [32, 256, 5120], P('gz', None, 'gx'), may hold values from -200 to 200, as said below
- flags: int32 [32, 2], P('gz'), may hold values 0 or 1
- offsets: int32 [32, 1, 128, 2], P('gz', None, 'gx'), may hold values from -40 to 40
Outputs:
- corr_near: float32 [32, 1, 128, 128, 128], P('gz', None, 'gx')
- corr_far: float32 [32, 1, 128, 128, 128], P('gz', None, 'gx')
The draws below stay inside these ranges and needn't reach their ends.
Inputs may be any that keep to these rules, and one draw needn't show every extreme that they name: `image`: pixel intensities.
All inputs are finite; a program needn't handle non-finite values. No bound on the sum of `flags` on one device may be relied on, other than what follows from the above.
Results may differ from the reference program's by a relative error of at most 0.009.
Values may be sent and summed in bfloat16 or wider, within the bound.
A program may use at most 64 MiB of HBM per device.

```python
import math
import jax
import jax.numpy as jnp
from jax import lax

P_SIZE = 256
STRIDE = 40
OFFMAX = 40
CROP = 128
PROWS = 1
HEIGHT = 256
PCOLS = 128
WIDTH = 5120
SECTIONS = 32


def draw_image(key, part):
    key = jax.random.fold_in(key, 5)
    base_key, row_key, col_key = jax.random.split(key, 3)
    row_scale = jnp.exp(jax.random.uniform(row_key, (SECTIONS, HEIGHT, 1), jnp.float32, 0.0, 2.3))
    col_scale = jnp.exp(jax.random.uniform(col_key, (SECTIONS, 1, WIDTH), jnp.float32, 0.0, 2.3))
    base = jnp.clip(jax.random.normal(base_key, (SECTIONS, HEIGHT, WIDTH), jnp.float32), -6.0, 6.0)
    return (base * row_scale * col_scale / 3.0).astype(jnp.bfloat16)


def plant(entries, stream_key, smallest, top_value):
    index_at = [jax.random.randint(jax.random.fold_in(stream_key, axis), (), 0, length) for axis, length in enumerate(entries.shape)]
    longest = entries.shape.index(max(entries.shape))
    neighbour = index_at[:longest] + [(index_at[longest] + 1) % entries.shape[longest]] + index_at[longest + 1:]
    return entries.at[tuple(index_at)].set(smallest).at[tuple(neighbour)].set(top_value)


def setup_inputs(seed: int = 0) -> dict:
    key_list = jax.random.split(jax.random.key(seed), 4)
    image = draw_image(jax.random.fold_in(key_list[3], 71), 0)
    flags = plant((jax.random.randint(key_list[1], (SECTIONS, 2), 0, 4) < 3).astype(jnp.int32), jax.random.fold_in(key_list[1], 1), 0, 1)
    offsets = plant(jax.random.randint(key_list[2], (SECTIONS, PROWS, PCOLS, 2), -OFFMAX, OFFMAX + 1), jax.random.fold_in(key_list[2], 1), -OFFMAX, OFFMAX).astype(jnp.int32)
    return {"image": image, "flags": flags, "offsets": offsets}


def tables(index, size):
    grid = jnp.arange(size, dtype=jnp.int32)
    phase = index[:, None] * grid[None, :] % size
    angle = phase.astype(jnp.float32) * (2.0 * math.pi / size)
    return (jnp.cos(angle).astype(jnp.bfloat16), jnp.sin(angle).astype(jnp.bfloat16))

def normalize(patches):
    values = patches.astype(jnp.float32)
    centred = values - lax.optimization_barrier(jnp.mean(values, axis=(1, 2), keepdims=True))
    factor = lax.rsqrt(lax.optimization_barrier(jnp.mean(centred * centred, axis=(1, 2), keepdims=True)) + 1e-05)
    return (centred * factor).astype(jnp.bfloat16)

def spectrum(normed, cos_f, sin_f):
    count = normed.shape[0]
    first = jnp.concatenate([cos_f, -sin_f], axis=1)
    rowwise = jnp.dot(normed.reshape(count * P_SIZE, P_SIZE), first, preferred_element_type=jnp.float32)
    rowwise = rowwise.astype(jnp.bfloat16).reshape(count, P_SIZE, 2 * P_SIZE)
    swapped = jnp.concatenate([rowwise[:, :, P_SIZE:], -rowwise[:, :, :P_SIZE]], axis=2)
    part_one = jnp.einsum('ly,byk->blk', cos_f.astype(jnp.float32), rowwise.astype(jnp.float32))
    part_two = jnp.einsum('ly,byk->blk', sin_f.astype(jnp.float32), swapped.astype(jnp.float32))
    return part_one + part_two

def correlate(first_spec, second_spec, cos_c, sin_c):
    scale = 1.0 / (P_SIZE * P_SIZE)
    a_re, a_im = (first_spec[:, :, :P_SIZE], first_spec[:, :, P_SIZE:])
    b_re, b_im = (second_spec[:, :, :P_SIZE], second_spec[:, :, P_SIZE:])
    cross_re = ((a_re * b_re + a_im * b_im) * scale).astype(jnp.bfloat16)
    cross_im = ((a_re * b_im - a_im * b_re) * scale).astype(jnp.bfloat16)
    cross = jnp.concatenate([cross_re, cross_im], axis=2).astype(jnp.float32)
    swapped = jnp.concatenate([-cross_im, cross_re], axis=2).astype(jnp.float32)
    inner = jnp.einsum('ul,blk->buk', cos_c.astype(jnp.float32), cross)
    inner = inner + jnp.einsum('ul,blk->buk', sin_c.astype(jnp.float32), swapped)
    inner = inner.astype(jnp.bfloat16).astype(jnp.float32)
    back = jnp.concatenate([cos_c, -sin_c], axis=1).astype(jnp.float32)
    return jnp.einsum('buk,vk->bvu', inner, back) / P_SIZE

def cut_patches(section, row_start, col_start):
    cut = jax.vmap(lambda top, left: lax.dynamic_slice(section, (top, left), (P_SIZE, P_SIZE)))(row_start, col_start)
    return jnp.swapaxes(cut, 1, 2)

def reference(image, flags, offsets):
    margin = P_SIZE - STRIDE + OFFMAX
    padded = jnp.pad(image, ((0, 2), (0, 0), (margin, margin)))
    cos_f, sin_f = tables(jnp.arange(P_SIZE, dtype=jnp.int32), P_SIZE)
    cos_c, sin_c = tables((jnp.arange(CROP, dtype=jnp.int32) - CROP // 2) % P_SIZE, P_SIZE)
    count = PROWS * PCOLS
    row_start = jnp.repeat(jnp.arange(PROWS, dtype=jnp.int32) * STRIDE, PCOLS)
    col_start = jnp.tile(margin + jnp.arange(PCOLS, dtype=jnp.int32) * STRIDE, PROWS)

    def one_section(index):
        moves = offsets[index].reshape(count, 2)
        own = cut_patches(padded[index], row_start, col_start)
        near = cut_patches(padded[index + 1], row_start, col_start + moves[:, 0])
        far = cut_patches(padded[index + 2], row_start, col_start + moves[:, 1])
        own_spec = spectrum(normalize(own), cos_f, sin_f)
        near_spec = spectrum(normalize(near), cos_f, sin_f)
        far_spec = spectrum(normalize(far), cos_f, sin_f)
        first = correlate(own_spec, near_spec, cos_c, sin_c) * flags[index, 0].astype(jnp.float32)
        second = correlate(own_spec, far_spec, cos_c, sin_c) * flags[index, 1].astype(jnp.float32)
        return (first.reshape(PROWS, PCOLS, CROP, CROP), second.reshape(PROWS, PCOLS, CROP, CROP))
    corr_near, corr_far = lax.map(one_section, jnp.arange(SECTIONS, dtype=jnp.int32))
    return (corr_near, corr_far)
```

```python
import jax
import jax.numpy as jnp
import numpy as np
from jax import lax
from jax.experimental import pallas as pl
from jax.experimental.pallas import tpu as pltpu
from jax.sharding import PartitionSpec as P

P_SIZE = 256
STRIDE = 40
OFFMAX = 40
CROP = 128
HALF = P_SIZE // 2
LOW = 48
HIGH = 256
MESH = pl.DeviceIdType.MESH
F32 = jnp.float32
BF16 = jnp.bfloat16


def transform_tables():
    n = np.arange(P_SIZE)
    k = np.arange(HALF)
    angle = 2.0 * np.pi / P_SIZE
    full = np.zeros((P_SIZE, P_SIZE))
    full[:HALF] = np.cos(angle * ((k[:, None] * n[None]) % P_SIZE))
    full[HALF:] = np.sin(angle * ((k[:, None] * n[None]) % P_SIZE))
    full[HALF] = 1.0 - 2.0 * (n % 2)
    shifts = (np.arange(CROP) - CROP // 2) % P_SIZE
    crop = full[:, shifts].T.copy()
    crop[:, 0] *= 0.5
    crop[:, HALF] *= 0.5
    return full.astype(jnp.bfloat16), crop.astype(jnp.bfloat16)


def rows_to_spectrum_y(ext_ref, ext_row, y_ref, y_row, count, full_ref, step=208):
    done = 0
    while done < count:
        size = min(step, count - done)
        values = lax.dot_general(
            ext_ref[ext_row + done : ext_row + done + size, :],
            full_ref[...],
            (((1,), (1,)), ((), ())),
            preferred_element_type=F32,
        )
        y_ref[0, y_row + done : y_row + done + size, :] = values[:, :HALF]
        y_ref[1, y_row + done : y_row + done + size, :] = values[:, HALF:]
        done += size


def patch_spectrum(y_ref, start, full_ref):
    lane = lax.broadcasted_iota(jnp.int32, (1, HALF), 1)
    left = y_ref[0, pl.ds(start, P_SIZE), :]
    right = y_ref[1, pl.ds(start, P_SIZE), :]
    mean = jnp.where(lane == 0, jnp.sum(left, axis=0, keepdims=True) * (1.0 / P_SIZE), 0.0)
    left = left - mean
    energy = jnp.sum(left * left + right * right, axis=0, keepdims=True)
    energy = energy * jnp.where(lane == 0, 1.0, 2.0)
    variance = jnp.sum(energy, axis=1, keepdims=True) * (1.0 / (P_SIZE * P_SIZE * P_SIZE))
    factor = lax.rsqrt(variance + 1e-5)
    values = jnp.concatenate([left.astype(BF16), right.astype(BF16)], axis=1)
    return jnp.dot(full_ref[...], values, preferred_element_type=F32), factor


def cross_rows(a, b, r_ref, row, size):
    lane0 = lax.broadcasted_iota(jnp.int32, (size, HALF), 1) == 0
    p, u, v, t = a(0, 0), a(0, 1), a(1, 0), a(1, 1)
    bp, bu, bv, bt = b(0, 0), b(0, 1), b(1, 0), b(1, 1)
    pp, vv, uu, tt = p * bp, v * bv, u * bu, t * bt
    pu = p * bu - u * bp
    vt = v * bt - t * bv
    same = uu + tt
    turn = u * bt - t * bu
    even_r = pp + vv + jnp.where(lane0, 0.0, same)
    odd_i = p * bv - v * bp + jnp.where(lane0, 0.0, turn)
    even_i = jnp.where(lane0, same, pu + vt)
    odd_r = jnp.where(lane0, turn, p * bt + t * bp - u * bv - v * bu)
    if row == 0:
        row0 = lax.broadcasted_iota(jnp.int32, (size, HALF), 0) == 0
        even_r = jnp.where(row0, pp + jnp.where(lane0, 0.0, uu), even_r)
        odd_i = jnp.where(row0, vv + jnp.where(lane0, 0.0, tt), odd_i)
        even_i = jnp.where(row0, jnp.where(lane0, uu, pu), even_i)
        odd_r = jnp.where(row0, jnp.where(lane0, tt, vt), odd_r)
    r_ref[row : row + size, 0:HALF] = even_r.astype(BF16)
    r_ref[row : row + size, HALF:P_SIZE] = even_i.astype(BF16)
    r_ref[HALF + row : HALF + row + size, 0:HALF] = odd_i.astype(BF16)
    r_ref[HALF + row : HALF + row + size, HALF:P_SIZE] = odd_r.astype(BF16)


def pair_window(own_ref, index, other_ref, r_ref, crop_ref, scale):
    size = 16
    for row in range(0, HALF, size):

        def own(part, side, row=row):
            return own_ref[index, HALF * part + row : HALF * part + row + size, HALF * side : HALF * (side + 1)]

        def other(part, side, row=row):
            return other_ref[HALF * part + row : HALF * part + row + size, HALF * side : HALF * (side + 1)]

        cross_rows(own, other, r_ref, row, size)
    inner = jnp.dot(crop_ref[...], r_ref[...], preferred_element_type=F32).astype(BF16)
    window = lax.dot_general(
        crop_ref[...], inner, (((1,), (1,)), ((), ())), preferred_element_type=F32
    )
    return window * scale


def kernel(
    depth, width, off_ref, flag_ref, image_ref, full_ref, crop_ref, near_ref, far_ref,
    own, part, y_own, y_part, spec_own, spec_part, fac_own, cross, send_sem, recv_sem,
):
    z = lax.axis_index("gz")
    s = lax.axis_index("gx")
    strip = image_ref.shape[0]
    top = LOW + strip
    total = top + HIGH
    count = off_ref.shape[0]
    odd = lax.rem(z, 2) == 1
    even = jnp.logical_not(odd)
    has_left, has_right = s > 0, s < width - 1
    sec1, sec2 = z < depth - 1, z < depth - 2
    above = z >= 2
    both = jnp.logical_and

    mid, left, right = pl.ds(LOW, strip), pl.ds(0, LOW), pl.ds(top, HIGH)
    head, tail = pl.ds(LOW, HIGH), pl.ds(top - LOW, LOW)

    def copy(src, dst, slot, where):
        return pltpu.make_async_remote_copy(
            src_ref=src, dst_ref=dst, send_sem=send_sem.at[slot], recv_sem=recv_sem.at[slot],
            device_id=where, device_id_type=MESH,
        )

    here = own.at[mid]
    near, far = part.at[0], part.at[1]
    mate = jnp.where(odd, z - 1, z + 1)
    own_right = (has_left, has_right, copy(own.at[head], own.at[right], 0, (z, s - 1)))
    own_left = (
        both(odd, has_right),
        both(odd, has_left),
        copy(own.at[tail], own.at[left], 1, (z, s + 1)),
    )
    far_mid = (above, sec2, copy(here, far.at[mid], 2, (z - 2, s)))
    far_right = (
        both(above, has_left),
        both(sec2, has_right),
        copy(own.at[head], far.at[right], 3, (z - 2, s - 1)),
    )
    far_left = (
        both(above, has_right),
        both(sec2, has_left),
        copy(own.at[tail], far.at[left], 4, (z - 2, s + 1)),
    )
    gives = jnp.logical_or(odd, sec2)
    takes = jnp.logical_or(even, sec1)

    def start(condition, what):
        @pl.when(condition)
        def _():
            what.start()

    def arrive(condition, what):
        @pl.when(condition)
        def _():
            what.wait_recv()

    barrier = pltpu.get_barrier_semaphore()
    senders = (
        (has_right, (z, s + 1)),
        (both(odd, has_left), (z, s - 1)),
        (sec2, (z + 2, s)),
        (both(sec2, has_right), (z + 2, s + 1)),
        (both(sec2, has_left), (z + 2, s - 1)),
        (takes, (mate, s)),
    )
    for condition, where in senders:

        @pl.when(condition)
        def _(where=where):
            pl.semaphore_signal(barrier, inc=1, device_id=where, device_id_type=MESH)

    own[LOW:top, :] = image_ref[...]
    receivers = [c[0] for c in (own_right, own_left, far_mid, far_right, far_left)] + [gives]
    pl.semaphore_wait(barrier, sum(c.astype(jnp.int32) for c in receivers))

    for sends, _, what in (far_right, own_right, far_mid, far_left, own_left):
        start(sends, what)
    near_mid = copy(here, near.at[mid], 5, (mate, s))
    near_right = copy(own.at[right], near.at[right], 6, (mate, s))
    near_left = copy(own.at[left], near.at[left], 7, (mate, s))
    pass_mid = copy(far.at[mid], near.at[mid], 5, (mate, s))
    pass_right = copy(far.at[right], near.at[right], 6, (mate, s))
    pass_left = copy(far.at[left], near.at[left], 7, (mate, s))
    start(odd, near_mid)

    def clear(condition, ref, rows):
        @pl.when(condition)
        def _():
            ref[rows, :] = jnp.zeros((rows.size, P_SIZE), BF16)

    no = jnp.logical_not
    clear(no(has_right), own, right)
    clear(no(sec2), far, mid)
    clear(no(both(sec2, has_right)), far, right)
    clear(no(both(sec2, has_left)), far, left)
    clear(no(takes), near, mid)
    clear(no(both(takes, has_right)), near, right)
    clear(no(both(takes, has_left)), near, left)

    rows_to_spectrum_y(own, LOW, y_own, 0, strip, full_ref, 160)
    arrive(*own_right[1:])
    start(both(odd, has_right), near_right)
    arrive(*own_left[1:])
    start(both(odd, has_left), near_left)
    rows_to_spectrum_y(own, top, y_own, strip, y_own.shape[1] - strip, full_ref, 224)

    def own_patch(c, carry):
        spec_own[c], factor = patch_spectrum(y_own, c * STRIDE, full_ref)
        fac_own[pl.ds(c, 1), :] = jnp.broadcast_to(factor, (1, CROP))
        return carry

    lax.fori_loop(0, count, own_patch, 0)

    def one_partner(which, middle):
        rows_to_spectrum_y(part.at[which], 0, y_part, 0, total, full_ref)
        if middle is not None:
            middle()
        flag = flag_ref[0, which].astype(F32) * (4.0 / (P_SIZE * P_SIZE * P_SIZE))

        def pair(c, carry):
            start_row = LOW + c * STRIDE + off_ref[c, which]
            spec_part[...], factor = patch_spectrum(y_part, start_row, full_ref)
            scale = fac_own[pl.ds(c, 1), :] * factor * flag
            window = pair_window(spec_own, c, spec_part, cross, crop_ref, scale)

            @pl.when(which == 0)
            def _():
                near_ref[c] = window

            @pl.when(which == 1)
            def _():
                far_ref[c] = window

            return carry

        lax.fori_loop(0, count, pair, 0)

    def wait_far(condition):
        for _, gets, what in (far_mid, far_left, far_right):
            arrive(both(condition, gets), what)

    def wait_near(condition):
        arrive(both(condition, takes), near_mid)
        arrive(both(condition, both(takes, has_left)), near_left)
        arrive(both(condition, both(takes, has_right)), near_right)

    def hand_on():
        wait_far(even)
        start(both(even, sec2), pass_mid)
        start(both(even, both(sec2, has_left)), pass_left)
        start(both(even, both(sec2, has_right)), pass_right)

    first = jnp.where(odd, 1, 0)
    wait_near(even)
    wait_far(odd)
    one_partner(first, hand_on)
    wait_near(odd)
    one_partner(1 - first, None)

    for sends, _, what in (own_right, own_left, far_mid, far_right, far_left):

        @pl.when(sends)
        def _(what=what):
            what.wait_send()

    for condition, what in (
        (gives, near_mid),
        (both(gives, has_right), near_right),
        (both(gives, has_left), near_left),
    ):

        @pl.when(condition)
        def _(what=what):
            what.wait_send()


def solution(mesh):
    depth, width = mesh.shape["gz"], mesh.shape["gx"]
    full, crop = transform_tables()

    def on_device(image, flags, offsets):
        count = offsets.shape[2]
        strip = image.shape[2]
        total = LOW + strip + HIGH
        vmem = pl.BlockSpec(memory_space=pltpu.VMEM)
        smem = pl.BlockSpec(memory_space=pltpu.SMEM)
        window = jax.ShapeDtypeStruct((count, CROP, CROP), F32)

        def body(*refs):
            kernel(depth, width, *refs)

        near, far = pl.pallas_call(
            body,
            out_shape=[window, window],
            in_specs=[smem, smem, vmem, vmem, vmem],
            out_specs=[vmem, vmem],
            scratch_shapes=[
                pltpu.VMEM((total, P_SIZE), BF16),
                pltpu.VMEM((2, total, P_SIZE), BF16),
                pltpu.VMEM((2, 544, HALF), F32),
                pltpu.VMEM((2, total, HALF), F32),
                pltpu.VMEM((count, P_SIZE, P_SIZE), F32),
                pltpu.VMEM((P_SIZE, P_SIZE), F32),
                pltpu.VMEM((count, CROP), F32),
                pltpu.VMEM((P_SIZE, P_SIZE), BF16),
                pltpu.SemaphoreType.DMA((8,)),
                pltpu.SemaphoreType.DMA((8,)),
            ],
            compiler_params=pltpu.CompilerParams(
                collective_id=0, has_side_effects=True, vmem_limit_bytes=40 * 2**20
            ),
        )(offsets.reshape(count, 2), flags, jnp.transpose(image[0]), jnp.asarray(full), jnp.asarray(crop))
        shape = (1, 1, count, CROP, CROP)
        return near.reshape(shape), far.reshape(shape)

    in_specs = (P("gz", None, "gx"), P("gz", None), P("gz", None, "gx", None))
    out_specs = (P("gz", None, "gx", None, None), P("gz", None, "gx", None, None))
    return jax.shard_map(
        on_device, mesh=mesh, in_specs=in_specs, out_specs=out_specs, check_vma=False
    )
```

```python
import jax
import jax.numpy as jnp
import numpy as np
from jax import lax
from jax.experimental import pallas as pl
from jax.experimental.pallas import tpu as pltpu
from jax.sharding import PartitionSpec as P

P_SIZE = 256
STRIDE = 40
OFFMAX = 40
CROP = 128
HALF = P_SIZE // 2
LOW = 48
HIGH = 256
MESH = pl.DeviceIdType.MESH
F32 = jnp.float32
BF16 = jnp.bfloat16


def transform_tables():
    n = np.arange(P_SIZE)
    k = np.arange(HALF)
    angle = 2.0 * np.pi / P_SIZE
    full = np.zeros((P_SIZE, P_SIZE))
    full[:HALF] = np.cos(angle * ((k[:, None] * n[None]) % P_SIZE))
    full[HALF:] = np.sin(angle * ((k[:, None] * n[None]) % P_SIZE))
    full[HALF] = 1.0 - 2.0 * (n % 2)
    shifts = (np.arange(CROP) - CROP // 2) % P_SIZE
    crop = full[:, shifts].T.copy()
    crop[:, 0] *= 0.5
    crop[:, HALF] *= 0.5
    return full.astype(jnp.bfloat16), crop.astype(jnp.bfloat16)


def rows_to_spectrum_y(ext_ref, ext_row, y_ref, y_row, count, full_ref, step=208):
    done = 0
    while done < count:
        size = min(step, count - done)
        values = lax.dot_general(
            ext_ref[ext_row + done : ext_row + done + size, :],
            full_ref[...],
            (((1,), (1,)), ((), ())),
            preferred_element_type=F32,
        )
        y_ref[0, y_row + done : y_row + done + size, :] = values[:, :HALF]
        y_ref[1, y_row + done : y_row + done + size, :] = values[:, HALF:]
        done += size


def patch_spectrum(y_ref, start, full_ref):
    lane = lax.broadcasted_iota(jnp.int32, (1, HALF), 1)
    left = y_ref[0, pl.ds(start, P_SIZE), :]
    right = y_ref[1, pl.ds(start, P_SIZE), :]
    mean = jnp.where(lane == 0, jnp.sum(left, axis=0, keepdims=True) * (1.0 / P_SIZE), 0.0)
    left = left - mean
    energy = jnp.sum(left * left + right * right, axis=0, keepdims=True)
    energy = energy * jnp.where(lane == 0, 1.0, 2.0)
    variance = jnp.sum(energy, axis=1, keepdims=True) * (1.0 / (P_SIZE * P_SIZE * P_SIZE))
    factor = lax.rsqrt(variance + 1e-5)
    values = jnp.concatenate([left.astype(BF16), right.astype(BF16)], axis=1)
    return jnp.dot(full_ref[...], values, preferred_element_type=F32), factor


def cross_rows(a, b, r_ref, row, size):
    lane0 = lax.broadcasted_iota(jnp.int32, (size, HALF), 1) == 0
    p, u, v, t = a(0, 0), a(0, 1), a(1, 0), a(1, 1)
    bp, bu, bv, bt = b(0, 0), b(0, 1), b(1, 0), b(1, 1)
    pp, vv, uu, tt = p * bp, v * bv, u * bu, t * bt
    pu = p * bu - u * bp
    vt = v * bt - t * bv
    same = uu + tt
    turn = u * bt - t * bu
    even_r = pp + vv + jnp.where(lane0, 0.0, same)
    odd_i = p * bv - v * bp + jnp.where(lane0, 0.0, turn)
    even_i = jnp.where(lane0, same, pu + vt)
    odd_r = jnp.where(lane0, turn, p * bt + t * bp - u * bv - v * bu)
    if row == 0:
        row0 = lax.broadcasted_iota(jnp.int32, (size, HALF), 0) == 0
        even_r = jnp.where(row0, pp + jnp.where(lane0, 0.0, uu), even_r)
        odd_i = jnp.where(row0, vv + jnp.where(lane0, 0.0, tt), odd_i)
        even_i = jnp.where(row0, jnp.where(lane0, uu, pu), even_i)
        odd_r = jnp.where(row0, jnp.where(lane0, tt, vt), odd_r)
    r_ref[row : row + size, 0:HALF] = even_r.astype(BF16)
    r_ref[row : row + size, HALF:P_SIZE] = even_i.astype(BF16)
    r_ref[HALF + row : HALF + row + size, 0:HALF] = odd_i.astype(BF16)
    r_ref[HALF + row : HALF + row + size, HALF:P_SIZE] = odd_r.astype(BF16)


def cross_power(own_ref, other_ref, index, r_ref):
    size = 16
    for row in range(0, HALF, size):

        def own(part, side, row=row):
            return own_ref[index, HALF * part + row : HALF * part + row + size, HALF * side : HALF * (side + 1)]

        def other(part, side, row=row):
            return other_ref[index, HALF * part + row : HALF * part + row + size, HALF * side : HALF * (side + 1)]

        cross_rows(own, other, r_ref.at[index], row, size)


def crop_window(crop_ref, r_ref, index, scale):
    inner = jnp.dot(crop_ref[...], r_ref[index], preferred_element_type=F32).astype(BF16)
    window = lax.dot_general(
        crop_ref[...], inner, (((1,), (1,)), ((), ())), preferred_element_type=F32
    )
    return window * scale


def exchange_kernel(
    depth, width, off_hbm, flag_hbm, image_hbm, full_hbm, crop_hbm, window_ref, r_second, scale_second, crop_out,
    own, part, y_own, y_part, spec_own, spec_part, r_first, full_ref, off_ref, flag_ref,
    send_sem, recv_sem, local_sem, ready_sem,
):
    z = lax.axis_index("gz")
    s = lax.axis_index("gx")
    strip = image_hbm.shape[0]
    top = LOW + strip
    total = top + HIGH
    count = off_ref.shape[1]
    odd = lax.rem(z, 2) == 1
    even = jnp.logical_not(odd)
    has_left, has_right = s > 0, s < width - 1
    sec1, sec2 = z < depth - 1, z < depth - 2
    above = z >= 2
    both = jnp.logical_and
    no = jnp.logical_not
    half = depth // 2
    early = both(z >= half, z < half + 2)
    late = both(z >= half - 2, z < half)

    mid, left, right = pl.ds(LOW, strip), pl.ds(0, LOW), pl.ds(top, HIGH)
    head, tail = pl.ds(LOW, HIGH), pl.ds(top - LOW, LOW)

    def copy(src, dst, slot, where):
        return pltpu.make_async_remote_copy(
            src_ref=src, dst_ref=dst, send_sem=send_sem.at[slot], recv_sem=recv_sem.at[slot],
            device_id=where, device_id_type=MESH,
        )

    here = own.at[mid]
    near, far = part.at[0], part.at[1]
    mate = jnp.where(odd, z - 1, z + 1)
    own_right = (has_left, has_right, copy(own.at[head], own.at[right], 0, (z, s - 1)))
    own_left = (
        both(odd, has_right),
        both(odd, has_left),
        copy(own.at[tail], own.at[left], 1, (z, s + 1)),
    )
    far_mid = (above, sec2, copy(here, far.at[mid], 2, (z - 2, s)))
    far_right = (
        both(above, has_left),
        both(sec2, has_right),
        copy(own.at[head], far.at[right], 3, (z - 2, s - 1)),
    )
    far_left = (
        both(above, has_right),
        both(sec2, has_left),
        copy(own.at[tail], far.at[left], 4, (z - 2, s + 1)),
    )
    gives = jnp.logical_or(odd, sec2)
    takes = jnp.logical_or(even, sec1)

    def start(condition, what):
        @pl.when(condition)
        def _():
            what.start()

    def arrive(condition, what):
        @pl.when(condition)
        def _():
            what.wait_recv()

    barrier = pltpu.get_barrier_semaphore()
    signals = (
        (has_right, (z, s + 1)),
        (both(odd, has_left), (z, s - 1)),
        (takes, (mate, s)),
        (both(sec2, no(late)), (z + 2, s)),
        (both(both(sec2, no(late)), has_right), (z + 2, s + 1)),
        (both(both(sec2, no(late)), has_left), (z + 2, s - 1)),
        (early, (z - 2, s)),
        (both(early, has_right), (z - 2, s + 1)),
        (both(early, has_left), (z - 2, s - 1)),
    )
    for condition, where in signals:

        @pl.when(condition)
        def _(where=where):
            pl.semaphore_signal(barrier, inc=1, device_id=where, device_id_type=MESH)

    loads = [
        pltpu.make_async_copy(src, dst, local_sem.at[i])
        for i, (src, dst) in enumerate((
            (image_hbm, here), (full_hbm, full_ref), (crop_hbm, crop_out), (off_hbm, off_ref), (flag_hbm, flag_ref)
        ))
    ]
    for load in loads:
        load.start()

    def clear(condition, ref, rows):
        @pl.when(condition)
        def _():
            ref[rows, :] = jnp.zeros((rows.size, P_SIZE), BF16)

    clear(no(has_right), own, right)
    clear(no(sec2), far, mid)
    clear(no(both(sec2, has_right)), far, right)
    clear(no(both(sec2, has_left)), far, left)
    clear(no(takes), near, mid)
    clear(no(both(takes, has_right)), near, right)
    clear(no(both(takes, has_left)), near, left)

    def as_int(condition):
        return condition.astype(jnp.int32)

    three = 1 + as_int(has_left) + as_int(has_right)
    expected = as_int(has_left) + as_int(both(odd, has_right)) + as_int(gives)
    expected += jnp.where(both(above, no(early)), three, 0) + jnp.where(late, three, 0)
    loads[0].wait()
    pl.semaphore_wait(barrier, expected)

    for condition, where in (
        (late, (z + 2, s)),
        (both(late, has_right), (z + 2, s + 1)),
        (both(late, has_left), (z + 2, s - 1)),
    ):

        @pl.when(condition)
        def _(where=where):
            pl.semaphore_signal(ready_sem, inc=1, device_id=where, device_id_type=MESH)

    start(own_right[0], own_right[2])
    for sends, _, what in (far_right, far_mid, far_left):
        start(both(sends, no(early)), what)
    start(own_left[0], own_left[2])
    near_mid = copy(here, near.at[mid], 5, (mate, s))
    near_right = copy(own.at[right], near.at[right], 6, (mate, s))
    near_left = copy(own.at[left], near.at[left], 7, (mate, s))
    pass_mid = copy(far.at[mid], near.at[mid], 5, (mate, s))
    pass_right = copy(far.at[right], near.at[right], 6, (mate, s))
    pass_left = copy(far.at[left], near.at[left], 7, (mate, s))
    start(odd, near_mid)

    for load in loads[1:]:
        load.wait()
    rows_to_spectrum_y(own, LOW, y_own, 0, strip, full_ref, strip)
    arrive(*own_right[1:])
    start(both(odd, has_right), near_right)
    arrive(*own_left[1:])
    start(both(odd, has_left), near_left)
    rows_to_spectrum_y(own, top, y_own, strip, y_own.shape[1] - strip, full_ref, 224)

    fac_own = []
    for c in range(count):
        spec_own[c], factor = patch_spectrum(y_own, c * STRIDE, full_ref)
        fac_own.append(factor)

    @pl.when(early)
    def _():
        pl.semaphore_wait(ready_sem, three)

    for sends, _, what in (far_right, far_mid, far_left):
        start(both(sends, early), what)

    def one_partner(which, r_ref):
        for rows, size in ((0, top), (top, HIGH)):
            rows_to_spectrum_y(part.at[which], rows, y_part, rows, size, full_ref, 368)
        flag = flag_ref[0, which].astype(F32) * (4.0 / (P_SIZE * P_SIZE * P_SIZE))
        scales = []
        for c in range(count):
            start_row = LOW + c * STRIDE + off_ref[which, c]
            spec_part[c], factor = patch_spectrum(y_part, start_row, full_ref)
            scales.append(jnp.broadcast_to(fac_own[c] * factor * flag, (1, CROP)))
        for c in range(count):
            cross_power(spec_own, spec_part, c, r_ref)
        return scales

    def wait_far(condition):
        for _, gets, what in (far_mid, far_left, far_right):
            arrive(both(condition, gets), what)

    def wait_near(condition):
        arrive(both(condition, takes), near_mid)
        arrive(both(condition, both(takes, has_left)), near_left)
        arrive(both(condition, both(takes, has_right)), near_right)

    wait_far(sec2)
    start(both(even, sec2), pass_mid)
    start(both(even, both(sec2, has_left)), pass_left)
    start(both(even, both(sec2, has_right)), pass_right)
    first = as_int(odd)
    wait_near(even)
    scales = one_partner(first, r_first)
    for c in range(count):
        window_ref[c] = crop_window(crop_out, r_first, c, scales[c])
    wait_near(odd)
    scales = one_partner(1 - first, r_second)
    for c in range(count):
        scale_second[c : c + 1, :] = scales[c]

    for sends, _, what in (own_right, own_left, far_mid, far_right, far_left):

        @pl.when(sends)
        def _(what=what):
            what.wait_send()

    for condition, what in (
        (gives, near_mid),
        (both(gives, has_right), near_right),
        (both(gives, has_left), near_left),
    ):

        @pl.when(condition)
        def _(what=what):
            what.wait_send()


def finish_kernel(window_ref, r_ref, scale_ref, crop_ref, near_hbm, far_hbm, second, sem):
    odd = lax.rem(lax.axis_index("gz"), 2) == 1
    count = window_ref.shape[0]

    def put(source, one, other, slot):
        @pl.when(odd)
        def _():
            pltpu.make_async_copy(source, one, sem.at[slot]).start()

        @pl.when(jnp.logical_not(odd))
        def _():
            pltpu.make_async_copy(source, other, sem.at[slot]).start()

    put(window_ref, far_hbm, near_hbm, 0)
    for c in range(count):
        second[c] = crop_window(crop_ref, r_ref, c, scale_ref[c : c + 1, :])
        if c % 2 == 1:
            rows = pl.ds(c - 1, 2)
            put(second.at[rows], near_hbm.at[rows], far_hbm.at[rows], 1 + c // 2)
    pltpu.make_async_copy(window_ref, near_hbm, sem.at[0]).wait()
    for c in range(1, count, 2):
        rows = pl.ds(c - 1, 2)
        pltpu.make_async_copy(second.at[rows], near_hbm.at[rows], sem.at[1 + c // 2]).wait()


def solution(mesh):
    depth, width = mesh.shape["gz"], mesh.shape["gx"]
    full, crop = transform_tables()

    def on_device(image, flags, offsets):
        count = offsets.shape[2]
        strip = image.shape[2]
        total = LOW + strip + HIGH
        vmem = pl.BlockSpec(memory_space=pltpu.VMEM)
        hbm = pl.BlockSpec(memory_space=pltpu.HBM)
        window = jax.ShapeDtypeStruct((count, CROP, CROP), F32)
        spectra = jax.ShapeDtypeStruct((count, P_SIZE, P_SIZE), BF16)
        scale = jax.ShapeDtypeStruct((count, CROP), F32)

        def body(*refs):
            exchange_kernel(depth, width, *refs)

        first, cross, scales, table = pl.pallas_call(
            body,
            out_shape=[window, spectra, scale, jax.ShapeDtypeStruct((CROP, P_SIZE), BF16)],
            in_specs=[hbm] * 5,
            out_specs=[vmem] * 4,
            scratch_shapes=[
                pltpu.VMEM((total, P_SIZE), BF16),
                pltpu.VMEM((2, total, P_SIZE), BF16),
                pltpu.VMEM((2, 544, HALF), F32),
                pltpu.VMEM((2, total, HALF), F32),
                pltpu.VMEM((count, P_SIZE, P_SIZE), F32),
                pltpu.VMEM((count, P_SIZE, P_SIZE), F32),
                pltpu.VMEM((count, P_SIZE, P_SIZE), BF16),
                pltpu.VMEM((P_SIZE, P_SIZE), BF16),
                pltpu.SMEM((2, count), jnp.int32),
                pltpu.SMEM((1, 2), jnp.int32),
                pltpu.SemaphoreType.DMA((8,)),
                pltpu.SemaphoreType.DMA((8,)),
                pltpu.SemaphoreType.DMA((5,)),
                pltpu.SemaphoreType.REGULAR,
            ],
            name="exchange",
            compiler_params=pltpu.CompilerParams(
                collective_id=0, has_side_effects=True, vmem_limit_bytes=40 * 2**20
            ),
        )(*(
            pltpu.with_memory_space_constraint(operand, pltpu.HBM)
            for operand in (
                jnp.transpose(offsets[0, 0]), flags, jnp.transpose(image[0]), jnp.asarray(full), jnp.asarray(crop)
            )
        ))
        near, far = pl.pallas_call(
            finish_kernel,
            out_shape=[window, window],
            in_specs=[vmem] * 4,
            out_specs=[hbm] * 2,
            scratch_shapes=[
                pltpu.VMEM((count, CROP, CROP), F32),
                pltpu.SemaphoreType.DMA((1 + count // 2,)),
            ],
            name="finish",
            compiler_params=pltpu.CompilerParams(vmem_limit_bytes=16 * 2**20),
        )(first, cross, scales, table)
        shape = (1, 1, count, CROP, CROP)
        return near.reshape(shape), far.reshape(shape)

    in_specs = (P("gz", None, "gx"), P("gz", None), P("gz", None, "gx", None))
    out_specs = (P("gz", None, "gx", None, None), P("gz", None, "gx", None, None))
    return jax.shard_map(
        on_device, mesh=mesh, in_specs=in_specs, out_specs=out_specs, check_vma=False
    )
```

```python
import jax
import jax.numpy as jnp
import numpy as np
from jax import lax
from jax.experimental import pallas as pl
from jax.experimental.pallas import tpu as pltpu
from jax.sharding import PartitionSpec as P

P_SIZE = 256
STRIDE = 40
OFFMAX = 40
CROP = 128
HALF = P_SIZE // 2
LOW = 48
HIGH = 256
INNER = (1, 2, 3)
OUTER = (0, 4, 5, 6, 7)
MESH = pl.DeviceIdType.MESH
F32 = jnp.float32
BF16 = jnp.bfloat16


def transform_tables():
    n = np.arange(P_SIZE)
    k = np.arange(HALF)
    angle = 2.0 * np.pi / P_SIZE
    full = np.zeros((P_SIZE, P_SIZE))
    full[:HALF] = np.cos(angle * ((k[:, None] * n[None]) % P_SIZE))
    full[HALF:] = np.sin(angle * ((k[:, None] * n[None]) % P_SIZE))
    full[HALF] = 1.0 - 2.0 * (n % 2)
    shifts = (np.arange(CROP) - CROP // 2) % P_SIZE
    crop = full[:, shifts].T.copy()
    crop[:, 0] *= 0.5
    crop[:, HALF] *= 0.5
    return full.astype(jnp.bfloat16), crop.astype(jnp.bfloat16)


def rows_to_spectrum_y(ext_ref, ext_row, y_ref, y_row, count, full_ref, step=208):
    done = 0
    while done < count:
        size = min(step, count - done)
        values = lax.dot_general(
            ext_ref[ext_row + done : ext_row + done + size, :],
            full_ref[...],
            (((1,), (1,)), ((), ())),
            preferred_element_type=F32,
        )
        y_ref[0, y_row + done : y_row + done + size, :] = values[:, :HALF]
        y_ref[1, y_row + done : y_row + done + size, :] = values[:, HALF:]
        done += size


def patch_spectrum(y_ref, start, full_ref):
    lane = lax.broadcasted_iota(jnp.int32, (1, HALF), 1)
    left = y_ref[0, pl.ds(start, P_SIZE), :]
    right = y_ref[1, pl.ds(start, P_SIZE), :]
    mean = jnp.where(lane == 0, jnp.sum(left, axis=0, keepdims=True) * (1.0 / P_SIZE), 0.0)
    left = left - mean
    energy = jnp.sum(left * left + right * right, axis=0, keepdims=True)
    energy = energy * jnp.where(lane == 0, 1.0, 2.0)
    variance = jnp.sum(energy, axis=1, keepdims=True) * (1.0 / (P_SIZE * P_SIZE * P_SIZE))
    factor = lax.rsqrt(variance + 1e-5)
    values = jnp.concatenate([left.astype(BF16), right.astype(BF16)], axis=1)
    return jnp.dot(full_ref[...], values, preferred_element_type=F32), factor


def cross_rows(a, b, r_ref, row, size):
    lane0 = lax.broadcasted_iota(jnp.int32, (size, HALF), 1) == 0
    p, u, v, t = a(0, 0), a(0, 1), a(1, 0), a(1, 1)
    bp, bu, bv, bt = b(0, 0), b(0, 1), b(1, 0), b(1, 1)
    pp, vv, uu, tt = p * bp, v * bv, u * bu, t * bt
    pu = p * bu - u * bp
    vt = v * bt - t * bv
    same = uu + tt
    turn = u * bt - t * bu
    even_r = pp + vv + jnp.where(lane0, 0.0, same)
    odd_i = p * bv - v * bp + jnp.where(lane0, 0.0, turn)
    even_i = jnp.where(lane0, same, pu + vt)
    odd_r = jnp.where(lane0, turn, p * bt + t * bp - u * bv - v * bu)
    if row == 0:
        row0 = lax.broadcasted_iota(jnp.int32, (size, HALF), 0) == 0
        even_r = jnp.where(row0, pp + jnp.where(lane0, 0.0, uu), even_r)
        odd_i = jnp.where(row0, vv + jnp.where(lane0, 0.0, tt), odd_i)
        even_i = jnp.where(row0, jnp.where(lane0, uu, pu), even_i)
        odd_r = jnp.where(row0, jnp.where(lane0, tt, vt), odd_r)
    r_ref[row : row + size, 0:HALF] = even_r.astype(BF16)
    r_ref[row : row + size, HALF:P_SIZE] = even_i.astype(BF16)
    r_ref[HALF + row : HALF + row + size, 0:HALF] = odd_i.astype(BF16)
    r_ref[HALF + row : HALF + row + size, HALF:P_SIZE] = odd_r.astype(BF16)


def cross_power(own_ref, other_ref, index, r_ref):
    size = 16
    for row in range(0, HALF, size):

        def own(part, side, row=row):
            return own_ref[index, HALF * part + row : HALF * part + row + size, HALF * side : HALF * (side + 1)]

        def other(part, side, row=row):
            return other_ref[index, HALF * part + row : HALF * part + row + size, HALF * side : HALF * (side + 1)]

        cross_rows(own, other, r_ref.at[index], row, size)


def crop_window(crop_ref, r_ref, index, scale):
    inner = jnp.dot(crop_ref[...], r_ref[index], preferred_element_type=F32).astype(BF16)
    window = lax.dot_general(
        crop_ref[...], inner, (((1,), (1,)), ((), ())), preferred_element_type=F32
    )
    return window * scale


def exchange_kernel(
    depth, width, off_hbm, flag_hbm, image_hbm, full_hbm, crop_hbm, window_ref, r_second, scale_second, crop_out,
    own, part_ref, y_own, y_part, spec_own, spec_part, r_first, full_ref, off_ref, flag_ref,
    send_sem, recv_sem, local_sem, ready_sem,
):
    z = lax.axis_index("gz")
    s = lax.axis_index("gx")
    strip = image_hbm.shape[0]
    top = LOW + strip
    total = top + HIGH
    count = off_ref.shape[1]
    odd = lax.rem(z, 2) == 1
    even = jnp.logical_not(odd)
    has_left, has_right = s > 0, s < width - 1
    sec1, sec2 = z < depth - 1, z < depth - 2
    above = z >= 2
    both = jnp.logical_and
    no = jnp.logical_not
    half = depth // 2
    early = both(z >= half, z < half + 2)
    late = both(z >= half - 2, z < half)

    here, left = pl.ds(LOW, strip), pl.ds(0, LOW)
    low, high = pl.ds(LOW, HALF), pl.ds(LOW + HALF, strip - HALF)
    right_a, right_b = pl.ds(top, HALF), pl.ds(top + HALF, HALF)
    head_b, tail = pl.ds(LOW + HALF, HALF), pl.ds(top - LOW, LOW)
    pieces = (high, low, right_a, right_b, left)
    near, far = part_ref.at[0], part_ref.at[1]
    mate = (jnp.where(odd, z - 1, z + 1), s)
    before, after, back = (z, s - 1), (z, s + 1), (z - 2, s)
    gives = jnp.logical_or(odd, sec2)
    takes = jnp.logical_or(even, sec1)

    def copy(condition, src, rows, dst, to_rows, send_slot, recv_slot, where):
        what = pltpu.make_async_remote_copy(
            src_ref=src.at[rows], dst_ref=dst.at[to_rows], send_sem=send_sem.at[send_slot],
            recv_sem=recv_sem.at[recv_slot], device_id=where, device_id_type=MESH,
        )
        return condition, what

    own_right_a = copy(has_left, own, low, own, right_a, 0, 0, before)
    own_right_b = copy(has_left, own, head_b, own, right_b, 1, 1, before)
    own_left = copy(has_right, own, tail, own, left, 2, 2, after)
    far_high = copy(above, own, high, far, high, 3, 3, back)
    far_low = copy(above, own, low, far, low, 4, 4, back)
    far_right_a = copy(both(above, has_right), own, right_a, far, right_a, 5, 5, back)
    far_right_b = copy(both(sec2, has_left), far, head_b, far, right_b, 7, 6, before)
    far_left = copy(both(sec2, has_right), far, tail, far, left, 8, 7, after)
    beside = (True, True, has_right, has_right, has_left)

    def hand(condition, source):
        return [
            copy(both(condition, side), source, rows, near, rows, 9 + n, 8 + n, mate)
            for n, (rows, side) in enumerate(zip(pieces, beside))
        ]

    give_own, give_far = hand(odd, own), hand(both(even, sec2), far)

    def start(what, condition=True):
        @pl.when(both(what[0], condition))
        def _():
            what[1].start()

    def arrive(what, condition):
        @pl.when(condition)
        def _():
            what[1].wait_recv()

    barrier = pltpu.get_barrier_semaphore()
    signals = (
        (both(sec2, no(late)), (z + 2, s)),
        (early, back),
        (has_right, after),
        (has_left, before),
        (takes, mate),
    )
    for condition, where in signals:

        @pl.when(condition)
        def _(where=where):
            pl.semaphore_signal(barrier, inc=1, device_id=where, device_id_type=MESH)

    loads = [
        pltpu.make_async_copy(src, dst, local_sem.at[i])
        for i, (src, dst) in enumerate((
            (image_hbm, own.at[here]), (full_hbm, full_ref), (crop_hbm, crop_out), (off_hbm, off_ref), (flag_hbm, flag_ref)
        ))
    ]
    for load in loads:
        load.start()

    def clear(condition, ref, rows):
        @pl.when(condition)
        def _():
            ref[rows, :] = jnp.zeros((rows.size, P_SIZE), BF16)

    for rows, side in zip(pieces, beside):
        if side is not True:
            clear(no(side), own, rows)
        clear(no(both(sec2, side)), far, rows)
        clear(no(both(takes, side)), near, rows)

    def as_int(condition):
        return condition.astype(jnp.int32)

    expected = as_int(has_left) + as_int(has_right) + as_int(gives)
    expected += as_int(both(above, no(early))) + as_int(late)
    loads[0].wait()
    pl.semaphore_wait(barrier, expected)

    @pl.when(late)
    def _():
        pl.semaphore_signal(ready_sem, inc=1, device_id=(z + 2, s), device_id_type=MESH)

    start(own_right_a)
    start(far_high, no(early))
    start(own_right_b)
    start(far_low, no(early))
    start(own_left)
    start(give_own[0])
    start(give_own[1])

    for load in loads[1:]:
        load.wait()
    rows_to_spectrum_y(own, LOW, y_own, 0, strip, full_ref, strip)
    arrive(own_right_a, has_right)
    start(far_right_a, no(early))
    start(give_own[2])
    arrive(own_right_b, has_right)
    start(give_own[3])
    arrive(own_left, has_left)
    start(give_own[4])
    rows_to_spectrum_y(own, top, y_own, strip, y_own.shape[1] - strip, full_ref, 224)

    fac_own = []
    for c in range(count):
        spec_own[c], factor = patch_spectrum(y_own, c * STRIDE, full_ref)
        fac_own.append(factor)

    def to_y(which, rows, size):
        rows_to_spectrum_y(part_ref.at[which], rows, y_part.at[which], rows, size, full_ref, 320)

    def partner(which, patches, r_ref):
        flag = flag_ref[0, which].astype(F32) * (4.0 / (P_SIZE * P_SIZE * P_SIZE))
        scales = []
        for c in patches:
            start_row = LOW + c * STRIDE + off_ref[which, c]
            spec_part[c], factor = patch_spectrum(y_part.at[which], start_row, full_ref)
            scales.append(jnp.broadcast_to(fac_own[c] * factor * flag, (1, CROP)))
        for c in patches:
            cross_power(spec_own, spec_part, c, r_ref)
        return scales

    def windows(patches, scales):
        for c, scale in zip(patches, scales):
            window_ref[c] = crop_window(crop_out, r_first, c, scale)

    def keep(scales):
        for c in range(count):
            scale_second[c : c + 1, :] = scales[c]

    def send_late():
        @pl.when(early)
        def _():
            pl.semaphore_wait(ready_sem, 1)

        for what in (far_high, far_low, far_right_a):
            start(what, early)

    arrive(far_high, sec2)
    start(far_right_b)
    start(far_left)
    start(give_far[0])
    arrive(far_low, sec2)
    start(give_far[1])
    to_y(1, LOW, strip)
    arrive(give_own[0], takes)
    arrive(give_own[1], takes)
    to_y(0, LOW, strip)

    @pl.when(even)
    def _():
        arrive(give_own[2], has_right)
        arrive(give_own[3], has_right)
        arrive(give_own[4], has_left)
        to_y(0, 0, LOW)
        to_y(0, top, HIGH)
        windows(range(count), partner(0, range(count), r_first))
        send_late()
        arrive(far_right_a, both(sec2, has_right))
        start(give_far[2])
        to_y(1, top, HALF)
        arrive(far_right_b, both(sec2, has_right))
        start(give_far[3])
        arrive(far_left, both(sec2, has_left))
        start(give_far[4])
        to_y(1, 0, LOW)
        to_y(1, top + HALF, HIGH - HALF)
        keep(partner(1, range(count), r_second))

    @pl.when(odd)
    def _():
        arrive(far_right_a, both(sec2, has_right))
        to_y(1, top, HALF)
        windows(INNER, partner(1, INNER, r_first))
        send_late()
        arrive(far_right_b, both(sec2, has_right))
        arrive(far_left, both(sec2, has_left))
        to_y(1, 0, LOW)
        to_y(1, top + HALF, HIGH - HALF)
        windows(OUTER, partner(1, OUTER, r_first))
        arrive(give_far[2], both(takes, has_right))
        arrive(give_far[3], both(takes, has_right))
        arrive(give_far[4], both(takes, has_left))
        to_y(0, 0, LOW)
        to_y(0, top, HIGH)
        keep(partner(0, range(count), r_second))

    sent = [own_right_a, own_right_b, own_left, far_high, far_low, far_right_a, far_right_b, far_left]
    for n in range(len(pieces)):
        sent.append((jnp.logical_or(give_own[n][0], give_far[n][0]), give_own[n][1]))
    for condition, what in sent:

        @pl.when(condition)
        def _(what=what):
            what.wait_send()


def finish_kernel(window_ref, r_ref, scale_ref, crop_ref, near_hbm, far_hbm, second, sem):
    odd = lax.rem(lax.axis_index("gz"), 2) == 1
    count = window_ref.shape[0]
    group = 2

    def puts(copies):
        @pl.when(odd)
        def _():
            for source, rows, slot in copies:
                first = slot < count // group
                pltpu.make_async_copy(source, (far_hbm if first else near_hbm).at[rows], sem.at[slot]).start()

        @pl.when(jnp.logical_not(odd))
        def _():
            for source, rows, slot in copies:
                first = slot < count // group
                pltpu.make_async_copy(source, (near_hbm if first else far_hbm).at[rows], sem.at[slot]).start()

    rows = [pl.ds(c, group) for c in range(0, count, group)]
    puts([(window_ref.at[r], r, n) for n, r in enumerate(rows)])
    for c in range(count):
        second[c] = crop_window(crop_ref, r_ref, c, scale_ref[c : c + 1, :])
        if c % group == group - 1:
            n = c // group
            puts([(second.at[rows[n]], rows[n], count // group + n)])
    for n, r in enumerate(rows):
        pltpu.make_async_copy(window_ref.at[r], near_hbm.at[r], sem.at[n]).wait()
        pltpu.make_async_copy(second.at[r], near_hbm.at[r], sem.at[count // group + n]).wait()


def solution(mesh):
    depth, width = mesh.shape["gz"], mesh.shape["gx"]
    full, crop = transform_tables()

    def on_device(image, flags, offsets):
        count = offsets.shape[2]
        strip = image.shape[2]
        total = LOW + strip + HIGH
        vmem = pl.BlockSpec(memory_space=pltpu.VMEM)
        hbm = pl.BlockSpec(memory_space=pltpu.HBM)
        window = jax.ShapeDtypeStruct((count, CROP, CROP), F32)
        spectra = jax.ShapeDtypeStruct((count, P_SIZE, P_SIZE), BF16)
        scale = jax.ShapeDtypeStruct((count, CROP), F32)

        def body(*refs):
            exchange_kernel(depth, width, *refs)

        first, cross, scales, table = pl.pallas_call(
            body,
            out_shape=[window, spectra, scale, jax.ShapeDtypeStruct((CROP, P_SIZE), BF16)],
            in_specs=[hbm] * 5,
            out_specs=[vmem] * 4,
            scratch_shapes=[
                pltpu.VMEM((total, P_SIZE), BF16),
                pltpu.VMEM((2, total, P_SIZE), BF16),
                pltpu.VMEM((2, 544, HALF), F32),
                pltpu.VMEM((2, 2, total, HALF), F32),
                pltpu.VMEM((count, P_SIZE, P_SIZE), F32),
                pltpu.VMEM((count, P_SIZE, P_SIZE), F32),
                pltpu.VMEM((count, P_SIZE, P_SIZE), BF16),
                pltpu.VMEM((P_SIZE, P_SIZE), BF16),
                pltpu.SMEM((2, count), jnp.int32),
                pltpu.SMEM((1, 2), jnp.int32),
                pltpu.SemaphoreType.DMA((14,)),
                pltpu.SemaphoreType.DMA((13,)),
                pltpu.SemaphoreType.DMA((5,)),
                pltpu.SemaphoreType.REGULAR,
            ],
            name="exchange",
            compiler_params=pltpu.CompilerParams(
                collective_id=0, has_side_effects=True, vmem_limit_bytes=40 * 2**20
            ),
        )(*(
            pltpu.with_memory_space_constraint(operand, pltpu.HBM)
            for operand in (
                jnp.transpose(offsets[0, 0]), flags, jnp.transpose(image[0]), jnp.asarray(full), jnp.asarray(crop)
            )
        ))
        near, far = pl.pallas_call(
            finish_kernel,
            out_shape=[window, window],
            in_specs=[vmem] * 4,
            out_specs=[hbm] * 2,
            scratch_shapes=[
                pltpu.VMEM((count, CROP, CROP), F32),
                pltpu.SemaphoreType.DMA((count,)),
            ],
            name="finish",
            compiler_params=pltpu.CompilerParams(vmem_limit_bytes=16 * 2**20),
        )(first, cross, scales, table)
        shape = (1, 1, count, CROP, CROP)
        return near.reshape(shape), far.reshape(shape)

    in_specs = (P("gz", None, "gx"), P("gz", None), P("gz", None, "gx", None))
    out_specs = (P("gz", None, "gx", None, None), P("gz", None, "gx", None, None))
    return jax.shard_map(
        on_device, mesh=mesh, in_specs=in_specs, out_specs=out_specs, check_vma=False
    )
```

```python
import jax
import jax.numpy as jnp
import numpy as np
from jax import lax
from jax.experimental import pallas as pl
from jax.experimental.pallas import tpu as pltpu
from jax.sharding import PartitionSpec as P

P_SIZE = 256
STRIDE = 40
OFFMAX = 40
CROP = 128
HALF = P_SIZE // 2
LOW = 48
HIGH = 256
INNER = (1, 2, 3)
OUTER = (0, 4, 5, 6, 7)
MESH = pl.DeviceIdType.MESH
F32 = jnp.float32
BF16 = jnp.bfloat16


def transform_tables():
    n = np.arange(P_SIZE)
    k = np.arange(HALF)
    angle = 2.0 * np.pi / P_SIZE
    full = np.zeros((P_SIZE, P_SIZE))
    full[:HALF] = np.cos(angle * ((k[:, None] * n[None]) % P_SIZE))
    full[HALF:] = np.sin(angle * ((k[:, None] * n[None]) % P_SIZE))
    full[HALF] = 1.0 - 2.0 * (n % 2)
    shifts = (np.arange(CROP) - CROP // 2) % P_SIZE
    crop = full[:, shifts].T.copy()
    crop[:, 0] *= 0.5
    crop[:, HALF] *= 0.5
    return full.astype(jnp.bfloat16), crop.astype(jnp.bfloat16)


def rows_to_spectrum_y(ext_ref, ext_row, y_ref, y_row, count, full_ref, step=208):
    done = 0
    while done < count:
        size = min(step, count - done)
        values = lax.dot_general(
            ext_ref[ext_row + done : ext_row + done + size, :],
            full_ref[...],
            (((1,), (1,)), ((), ())),
            preferred_element_type=F32,
        )
        y_ref[0, y_row + done : y_row + done + size, :] = values[:, :HALF]
        y_ref[1, y_row + done : y_row + done + size, :] = values[:, HALF:]
        done += size


def patch_spectrum(y_ref, start, full_ref):
    lane = lax.broadcasted_iota(jnp.int32, (1, HALF), 1)
    left = y_ref[0, pl.ds(start, P_SIZE), :]
    right = y_ref[1, pl.ds(start, P_SIZE), :]
    mean = jnp.where(lane == 0, jnp.sum(left, axis=0, keepdims=True) * (1.0 / P_SIZE), 0.0)
    left = left - mean
    energy = jnp.sum(left * left + right * right, axis=0, keepdims=True)
    energy = energy * jnp.where(lane == 0, 1.0, 2.0)
    variance = jnp.sum(energy, axis=1, keepdims=True) * (1.0 / (P_SIZE * P_SIZE * P_SIZE))
    factor = lax.rsqrt(variance + 1e-5)
    values = jnp.concatenate([left.astype(BF16), right.astype(BF16)], axis=1)
    return jnp.dot(full_ref[...], values, preferred_element_type=F32), factor


def cross_rows(a, b, r_ref, row, size):
    lane0 = lax.broadcasted_iota(jnp.int32, (size, HALF), 1) == 0
    p, u, v, t = a(0, 0), a(0, 1), a(1, 0), a(1, 1)
    bp, bu, bv, bt = b(0, 0), b(0, 1), b(1, 0), b(1, 1)
    pp, vv, uu, tt = p * bp, v * bv, u * bu, t * bt
    pu = p * bu - u * bp
    vt = v * bt - t * bv
    same = uu + tt
    turn = u * bt - t * bu
    even_r = pp + vv + jnp.where(lane0, 0.0, same)
    odd_i = p * bv - v * bp + jnp.where(lane0, 0.0, turn)
    even_i = jnp.where(lane0, same, pu + vt)
    odd_r = jnp.where(lane0, turn, p * bt + t * bp - u * bv - v * bu)
    if row == 0:
        row0 = lax.broadcasted_iota(jnp.int32, (size, HALF), 0) == 0
        even_r = jnp.where(row0, pp + jnp.where(lane0, 0.0, uu), even_r)
        odd_i = jnp.where(row0, vv + jnp.where(lane0, 0.0, tt), odd_i)
        even_i = jnp.where(row0, jnp.where(lane0, uu, pu), even_i)
        odd_r = jnp.where(row0, jnp.where(lane0, tt, vt), odd_r)
    r_ref[row : row + size, 0:HALF] = even_r.astype(BF16)
    r_ref[row : row + size, HALF:P_SIZE] = even_i.astype(BF16)
    r_ref[HALF + row : HALF + row + size, 0:HALF] = odd_i.astype(BF16)
    r_ref[HALF + row : HALF + row + size, HALF:P_SIZE] = odd_r.astype(BF16)


def cross_power(own_ref, other_ref, index, r_ref):
    size = 16
    for row in range(0, HALF, size):

        def own(part, side, row=row):
            return own_ref[index, HALF * part + row : HALF * part + row + size, HALF * side : HALF * (side + 1)]

        def other(part, side, row=row):
            return other_ref[index, HALF * part + row : HALF * part + row + size, HALF * side : HALF * (side + 1)]

        cross_rows(own, other, r_ref.at[index], row, size)


def crop_window(crop_ref, r_ref, index, scale):
    inner = jnp.dot(crop_ref[...], r_ref[index], preferred_element_type=F32).astype(BF16)
    window = lax.dot_general(
        crop_ref[...], inner, (((1,), (1,)), ((), ())), preferred_element_type=F32
    )
    return window * scale


def exchange_kernel(
    depth, width, off_hbm, flag_hbm, image_hbm, full_hbm, crop_hbm, window_ref, r_second, scale_second, crop_out,
    own, part_ref, y_own, y_part, spec_own, spec_part, r_first, full_ref, off_ref, flag_ref,
    send_sem, recv_sem, local_sem, ready_sem,
):
    z = lax.axis_index("gz")
    s = lax.axis_index("gx")
    strip = image_hbm.shape[0]
    top = LOW + strip
    total = top + HIGH
    count = off_ref.shape[1]
    odd = lax.rem(z, 2) == 1
    even = jnp.logical_not(odd)
    has_left, has_right = s > 0, s < width - 1
    sec1, sec2 = z < depth - 1, z < depth - 2
    above = z >= 2
    both = jnp.logical_and
    no = jnp.logical_not
    half = depth // 2
    early = both(z >= half, z < half + 2)
    late = both(z >= half - 2, z < half)

    here, left = pl.ds(LOW, strip), pl.ds(0, LOW)
    low, high = pl.ds(LOW, HALF), pl.ds(LOW + HALF, strip - HALF)
    right_a, right_b = pl.ds(top, HALF), pl.ds(top + HALF, HALF)
    head_b, tail = pl.ds(LOW + HALF, HALF), pl.ds(top - LOW, LOW)
    pieces = (high, low, right_a, right_b, left)
    near, far = part_ref.at[0], part_ref.at[1]
    mate = (jnp.where(odd, z - 1, z + 1), s)
    before, after, back = (z, s - 1), (z, s + 1), (z - 2, s)
    gives = jnp.logical_or(odd, sec2)
    takes = jnp.logical_or(even, sec1)

    def copy(condition, src, rows, dst, to_rows, send_slot, recv_slot, where):
        what = pltpu.make_async_remote_copy(
            src_ref=src.at[rows], dst_ref=dst.at[to_rows], send_sem=send_sem.at[send_slot],
            recv_sem=recv_sem.at[recv_slot], device_id=where, device_id_type=MESH,
        )
        return condition, what

    own_right_a = copy(has_left, own, low, own, right_a, 0, 0, before)
    own_right_b = copy(has_left, own, head_b, own, right_b, 1, 1, before)
    own_left = copy(has_right, own, tail, own, left, 2, 2, after)
    far_high = copy(above, own, high, far, high, 3, 3, back)
    far_low = copy(above, own, low, far, low, 4, 4, back)
    far_right_a = copy(both(above, has_right), own, right_a, far, right_a, 5, 5, back)
    far_right_b = copy(both(sec2, has_left), far, head_b, far, right_b, 7, 6, before)
    far_left = copy(both(sec2, has_right), far, tail, far, left, 8, 7, after)
    beside = (True, True, has_right, has_right, has_left)

    def hand(condition, source):
        return [
            copy(both(condition, side), source, rows, near, rows, 9 + n, 8 + n, mate)
            for n, (rows, side) in enumerate(zip(pieces, beside))
        ]

    give_own, give_far = hand(odd, own), hand(both(even, sec2), far)
    pair = both(even, sec2)
    near_right_b = copy(both(pair, has_left), far, head_b, near, right_b, 12, 11, (z + 1, s - 1))
    near_left = copy(both(pair, has_right), far, tail, near, left, 13, 12, (z + 1, s + 1))

    def start(what, condition=True):
        @pl.when(both(what[0], condition))
        def _():
            what[1].start()

    def arrive(what, condition):
        @pl.when(condition)
        def _():
            what[1].wait_recv()

    barrier = pltpu.get_barrier_semaphore()
    signals = (
        (both(sec2, no(late)), (z + 2, s)),
        (early, back),
        (has_right, after),
        (has_left, before),
        (takes, mate),
        (both(both(odd, sec1), has_right), (z - 1, s + 1)),
        (both(both(odd, sec1), has_left), (z - 1, s - 1)),
    )
    for condition, where in signals:

        @pl.when(condition)
        def _(where=where):
            pl.semaphore_signal(barrier, inc=1, device_id=where, device_id_type=MESH)

    loads = [
        pltpu.make_async_copy(src, dst, local_sem.at[i])
        for i, (src, dst) in enumerate((
            (image_hbm, own.at[here]), (full_hbm, full_ref), (crop_hbm, crop_out), (off_hbm, off_ref), (flag_hbm, flag_ref)
        ))
    ]
    for load in loads:
        load.start()

    def clear(condition, ref, rows):
        @pl.when(condition)
        def _():
            ref[rows, :] = jnp.zeros((rows.size, P_SIZE), BF16)

    for rows, side in zip(pieces, beside):
        if side is not True:
            clear(no(side), own, rows)
        clear(no(both(sec2, side)), far, rows)
        clear(no(both(takes, side)), near, rows)

    def as_int(condition):
        return condition.astype(jnp.int32)

    expected = as_int(has_left) + as_int(has_right) + as_int(gives)
    expected += as_int(both(above, no(early))) + as_int(late)
    expected += as_int(both(pair, has_left)) + as_int(both(pair, has_right))
    loads[0].wait()
    pl.semaphore_wait(barrier, expected)

    @pl.when(late)
    def _():
        pl.semaphore_signal(ready_sem, inc=1, device_id=(z + 2, s), device_id_type=MESH)

    start(own_right_a)
    start(far_high, no(early))
    start(own_right_b)
    start(far_low, no(early))
    start(own_left)
    start(give_own[0])
    start(give_own[1])

    last = both(z == 0, s == 0)

    def pass_strip(condition):
        arrive(far_high, both(condition, sec2))
        for what in (far_right_b, near_right_b, far_left, near_left, give_far[0]):
            start(what, condition)
        arrive(far_low, both(condition, sec2))
        start(give_far[1], condition)

    for load in loads[1:]:
        load.wait()
    rows_to_spectrum_y(own, LOW, y_own, 0, strip, full_ref, strip)
    pass_strip(last)
    arrive(own_right_a, has_right)
    start(far_right_a, no(early))
    start(give_own[2])
    arrive(own_right_b, has_right)
    start(give_own[3])
    arrive(own_left, has_left)
    start(give_own[4])
    rows_to_spectrum_y(own, top, y_own, strip, y_own.shape[1] - strip, full_ref, 224)

    fac_own = []
    for c in range(count):
        spec_own[c], factor = patch_spectrum(y_own, c * STRIDE, full_ref)
        fac_own.append(factor)

    def to_y(which, rows, size):
        rows_to_spectrum_y(part_ref.at[which], rows, y_part.at[which], rows, size, full_ref, 320)

    def partner(which, patches, r_ref):
        flag = flag_ref[0, which].astype(F32) * (4.0 / (P_SIZE * P_SIZE * P_SIZE))
        scales = []
        for c in patches:
            start_row = LOW + c * STRIDE + off_ref[which, c]
            spec_part[c], factor = patch_spectrum(y_part.at[which], start_row, full_ref)
            scales.append(jnp.broadcast_to(fac_own[c] * factor * flag, (1, CROP)))
        for c in patches:
            cross_power(spec_own, spec_part, c, r_ref)
        return scales

    def windows(patches, scales):
        for c, scale in zip(patches, scales):
            window_ref[c] = crop_window(crop_out, r_first, c, scale)

    def keep(scales):
        for c in range(count):
            scale_second[c : c + 1, :] = scales[c]

    def send_late():
        @pl.when(early)
        def _():
            pl.semaphore_wait(ready_sem, 1)

        for what in (far_high, far_low, far_right_a):
            start(what, early)

    def pass_on(condition):
        arrive(far_right_a, both(condition, both(sec2, has_right)))
        start(give_far[2], condition)

    pass_strip(no(last))
    to_y(1, LOW, strip)
    arrive(give_own[0], takes)
    arrive(give_own[1], takes)
    to_y(0, LOW, strip)

    @pl.when(even)
    def _():
        arrive(give_own[2], has_right)
        arrive(give_own[3], has_right)
        arrive(give_own[4], has_left)
        to_y(0, 0, LOW)
        to_y(0, top, HIGH)
        pass_on(last)
        windows(range(count), partner(0, range(count), r_first))
        send_late()
        pass_on(no(last))
        to_y(1, top, HALF)
        arrive(far_right_b, both(sec2, has_right))
        arrive(far_left, both(sec2, has_left))
        to_y(1, 0, LOW)
        to_y(1, top + HALF, HIGH - HALF)
        keep(partner(1, range(count), r_second))

    @pl.when(odd)
    def _():
        arrive(far_right_a, both(sec2, has_right))
        to_y(1, top, HALF)
        windows(INNER, partner(1, INNER, r_first))
        send_late()
        arrive(far_right_b, both(sec2, has_right))
        arrive(far_left, both(sec2, has_left))
        to_y(1, 0, LOW)
        to_y(1, top + HALF, HIGH - HALF)
        windows(OUTER, partner(1, OUTER, r_first))
        arrive(give_far[2], both(takes, has_right))
        arrive(near_right_b, both(takes, has_right))
        arrive(near_left, both(takes, has_left))
        to_y(0, 0, LOW)
        to_y(0, top, HIGH)
        keep(partner(0, range(count), r_second))

    sent = [own_right_a, own_right_b, own_left, far_high, far_low, far_right_a, far_right_b, far_left]
    for n, far_give in enumerate((*give_far[:3], near_right_b, near_left)):
        sent.append((jnp.logical_or(give_own[n][0], far_give[0]), give_own[n][1]))
    for condition, what in sent:

        @pl.when(condition)
        def _(what=what):
            what.wait_send()


def finish_kernel(window_ref, r_ref, scale_ref, crop_ref, near_hbm, far_hbm, second, sem):
    odd = lax.rem(lax.axis_index("gz"), 2) == 1
    count = window_ref.shape[0]
    group = 2

    def puts(copies):
        @pl.when(odd)
        def _():
            for source, rows, slot in copies:
                first = slot < count // group
                pltpu.make_async_copy(source, (far_hbm if first else near_hbm).at[rows], sem.at[slot]).start()

        @pl.when(jnp.logical_not(odd))
        def _():
            for source, rows, slot in copies:
                first = slot < count // group
                pltpu.make_async_copy(source, (near_hbm if first else far_hbm).at[rows], sem.at[slot]).start()

    rows = [pl.ds(c, group) for c in range(0, count, group)]
    puts([(window_ref.at[r], r, n) for n, r in enumerate(rows)])
    for c in range(count):
        second[c] = crop_window(crop_ref, r_ref, c, scale_ref[c : c + 1, :])
        if c % group == group - 1:
            n = c // group
            puts([(second.at[rows[n]], rows[n], count // group + n)])
    for n, r in enumerate(rows):
        pltpu.make_async_copy(window_ref.at[r], near_hbm.at[r], sem.at[n]).wait()
        pltpu.make_async_copy(second.at[r], near_hbm.at[r], sem.at[count // group + n]).wait()


def solution(mesh):
    depth, width = mesh.shape["gz"], mesh.shape["gx"]
    full, crop = transform_tables()

    def on_device(image, flags, offsets):
        count = offsets.shape[2]
        strip = image.shape[2]
        total = LOW + strip + HIGH
        vmem = pl.BlockSpec(memory_space=pltpu.VMEM)
        hbm = pl.BlockSpec(memory_space=pltpu.HBM)
        window = jax.ShapeDtypeStruct((count, CROP, CROP), F32)
        spectra = jax.ShapeDtypeStruct((count, P_SIZE, P_SIZE), BF16)
        scale = jax.ShapeDtypeStruct((count, CROP), F32)

        def body(*refs):
            exchange_kernel(depth, width, *refs)

        first, cross, scales, table = pl.pallas_call(
            body,
            out_shape=[window, spectra, scale, jax.ShapeDtypeStruct((CROP, P_SIZE), BF16)],
            in_specs=[hbm] * 5,
            out_specs=[vmem] * 4,
            scratch_shapes=[
                pltpu.VMEM((total, P_SIZE), BF16),
                pltpu.VMEM((2, total, P_SIZE), BF16),
                pltpu.VMEM((2, 544, HALF), F32),
                pltpu.VMEM((2, 2, total, HALF), F32),
                pltpu.VMEM((count, P_SIZE, P_SIZE), F32),
                pltpu.VMEM((count, P_SIZE, P_SIZE), F32),
                pltpu.VMEM((count, P_SIZE, P_SIZE), BF16),
                pltpu.VMEM((P_SIZE, P_SIZE), BF16),
                pltpu.SMEM((2, count), jnp.int32),
                pltpu.SMEM((1, 2), jnp.int32),
                pltpu.SemaphoreType.DMA((14,)),
                pltpu.SemaphoreType.DMA((13,)),
                pltpu.SemaphoreType.DMA((5,)),
                pltpu.SemaphoreType.REGULAR,
            ],
            name="exchange",
            compiler_params=pltpu.CompilerParams(
                collective_id=0, has_side_effects=True, vmem_limit_bytes=40 * 2**20
            ),
        )(*(
            pltpu.with_memory_space_constraint(operand, pltpu.HBM)
            for operand in (
                jnp.transpose(offsets[0, 0]), flags, jnp.transpose(image[0]), jnp.asarray(full), jnp.asarray(crop)
            )
        ))
        near, far = pl.pallas_call(
            finish_kernel,
            out_shape=[window, window],
            in_specs=[vmem] * 4,
            out_specs=[hbm] * 2,
            scratch_shapes=[
                pltpu.VMEM((count, CROP, CROP), F32),
                pltpu.SemaphoreType.DMA((count,)),
            ],
            name="finish",
            compiler_params=pltpu.CompilerParams(vmem_limit_bytes=16 * 2**20),
        )(first, cross, scales, table)
        shape = (1, 1, count, CROP, CROP)
        return near.reshape(shape), far.reshape(shape)

    in_specs = (P("gz", None, "gx"), P("gz", None), P("gz", None, "gx", None))
    out_specs = (P("gz", None, "gx", None, None), P("gz", None, "gx", None, None))
    return jax.shard_map(
        on_device, mesh=mesh, in_specs=in_specs, out_specs=out_specs, check_vma=False
    )
```

```python
import jax
import jax.numpy as jnp
import numpy as np
from jax import lax
from jax.experimental import pallas as pl
from jax.experimental.pallas import tpu as pltpu
from jax.sharding import PartitionSpec as P

P_SIZE = 256
STRIDE = 40
OFFMAX = 40
CROP = 128
HALF = P_SIZE // 2
LOW = 48
HIGH = 256
INNER = (1, 2, 3)
OUTER = (0, 4, 5, 6, 7)
MESH = pl.DeviceIdType.MESH
F32 = jnp.float32
BF16 = jnp.bfloat16


def transform_tables():
    n = np.arange(P_SIZE)
    k = np.arange(HALF)
    angle = 2.0 * np.pi / P_SIZE
    full = np.zeros((P_SIZE, P_SIZE))
    full[:HALF] = np.cos(angle * ((k[:, None] * n[None]) % P_SIZE))
    full[HALF:] = np.sin(angle * ((k[:, None] * n[None]) % P_SIZE))
    full[HALF] = 1.0 - 2.0 * (n % 2)
    shifts = (np.arange(CROP) - CROP // 2) % P_SIZE
    crop = full[:, shifts].T.copy()
    crop[:, 0] *= 0.5
    crop[:, HALF] *= 0.5
    return full.astype(jnp.bfloat16), crop.astype(jnp.bfloat16)


def rows_to_spectrum_y(ext_ref, ext_row, y_ref, y_row, count, full_ref, step=208):
    done = 0
    while done < count:
        size = min(step, count - done)
        values = lax.dot_general(
            ext_ref[ext_row + done : ext_row + done + size, :],
            full_ref[...],
            (((1,), (1,)), ((), ())),
            preferred_element_type=F32,
        )
        y_ref[0, y_row + done : y_row + done + size, :] = values[:, :HALF]
        y_ref[1, y_row + done : y_row + done + size, :] = values[:, HALF:]
        done += size


def patch_spectrum(y_ref, start, full_ref):
    lane = lax.broadcasted_iota(jnp.int32, (1, HALF), 1)
    left = y_ref[0, pl.ds(start, P_SIZE), :]
    right = y_ref[1, pl.ds(start, P_SIZE), :]
    mean = jnp.where(lane == 0, jnp.sum(left, axis=0, keepdims=True) * (1.0 / P_SIZE), 0.0)
    left = left - mean
    energy = jnp.sum(left * left + right * right, axis=0, keepdims=True)
    energy = energy * jnp.where(lane == 0, 1.0, 2.0)
    variance = jnp.sum(energy, axis=1, keepdims=True) * (1.0 / (P_SIZE * P_SIZE * P_SIZE))
    factor = lax.rsqrt(variance + 1e-5)
    values = jnp.concatenate([left.astype(BF16), right.astype(BF16)], axis=1)
    return jnp.dot(full_ref[...], values, preferred_element_type=F32), factor


def cross_rows(a, b, r_ref, row, size):
    lane0 = lax.broadcasted_iota(jnp.int32, (size, HALF), 1) == 0
    p, u, v, t = a(0, 0), a(0, 1), a(1, 0), a(1, 1)
    bp, bu, bv, bt = b(0, 0), b(0, 1), b(1, 0), b(1, 1)
    pp, vv, uu, tt = p * bp, v * bv, u * bu, t * bt
    pu = p * bu - u * bp
    vt = v * bt - t * bv
    same = uu + tt
    turn = u * bt - t * bu
    even_r = pp + vv + jnp.where(lane0, 0.0, same)
    odd_i = p * bv - v * bp + jnp.where(lane0, 0.0, turn)
    even_i = jnp.where(lane0, same, pu + vt)
    odd_r = jnp.where(lane0, turn, p * bt + t * bp - u * bv - v * bu)
    if row == 0:
        row0 = lax.broadcasted_iota(jnp.int32, (size, HALF), 0) == 0
        even_r = jnp.where(row0, pp + jnp.where(lane0, 0.0, uu), even_r)
        odd_i = jnp.where(row0, vv + jnp.where(lane0, 0.0, tt), odd_i)
        even_i = jnp.where(row0, jnp.where(lane0, uu, pu), even_i)
        odd_r = jnp.where(row0, jnp.where(lane0, tt, vt), odd_r)
    r_ref[row : row + size, 0:HALF] = even_r.astype(BF16)
    r_ref[row : row + size, HALF:P_SIZE] = even_i.astype(BF16)
    r_ref[HALF + row : HALF + row + size, 0:HALF] = odd_i.astype(BF16)
    r_ref[HALF + row : HALF + row + size, HALF:P_SIZE] = odd_r.astype(BF16)


def cross_power(own_ref, other_ref, index, r_ref):
    size = 16
    for row in range(0, HALF, size):

        def own(part, side, row=row):
            return own_ref[index, HALF * part + row : HALF * part + row + size, HALF * side : HALF * (side + 1)]

        def other(part, side, row=row):
            return other_ref[index, HALF * part + row : HALF * part + row + size, HALF * side : HALF * (side + 1)]

        cross_rows(own, other, r_ref.at[index], row, size)


def crop_window(crop_ref, r_ref, index, scale):
    inner = jnp.dot(crop_ref[...], r_ref[index], preferred_element_type=F32).astype(BF16)
    window = lax.dot_general(
        crop_ref[...], inner, (((1,), (1,)), ((), ())), preferred_element_type=F32
    )
    return window * scale


def exchange_kernel(
    depth, width, off_hbm, flag_hbm, image_hbm, full_hbm, crop_hbm, window_ref, r_second, scale_second, crop_out,
    own, part_ref, y_own, y_part, spec_own, spec_part, r_first, full_ref, off_ref, flag_ref,
    send_sem, recv_sem, local_sem, ready_sem,
):
    z = lax.axis_index("gz")
    s = lax.axis_index("gx")
    strip = image_hbm.shape[0]
    top = LOW + strip
    total = top + HIGH
    count = off_ref.shape[1]
    odd = lax.rem(z, 2) == 1
    even = jnp.logical_not(odd)
    has_left, has_right = s > 0, s < width - 1
    sec1, sec2 = z < depth - 1, z < depth - 2
    above = z >= 2
    both = jnp.logical_and
    no = jnp.logical_not
    half = depth // 2
    early = both(z >= half, z < half + 2)
    late = both(z >= half - 2, z < half)

    here, left = pl.ds(LOW, strip), pl.ds(0, LOW)
    low, high, last_rows = pl.ds(LOW, HALF), pl.ds(LOW + HALF, HALF), pl.ds(LOW + P_SIZE, strip - P_SIZE)
    right_a, right_b = pl.ds(top, HALF), pl.ds(top + HALF, HALF)
    head_b, tail = high, pl.ds(top - LOW, LOW)
    pieces = (high, low, right_a, right_b, left, last_rows)
    near, far = part_ref.at[0], part_ref.at[1]
    mate = (jnp.where(odd, z - 1, z + 1), s)
    before, after, back = (z, s - 1), (z, s + 1), (z - 2, s)
    gives = jnp.logical_or(odd, sec2)
    takes = jnp.logical_or(even, sec1)

    def copy(condition, src, rows, dst, to_rows, send_slot, recv_slot, where):
        what = pltpu.make_async_remote_copy(
            src_ref=src.at[rows], dst_ref=dst.at[to_rows], send_sem=send_sem.at[send_slot],
            recv_sem=recv_sem.at[recv_slot], device_id=where, device_id_type=MESH,
        )
        return condition, what

    own_right_a = copy(has_left, own, low, own, right_a, 0, 0, before)
    own_right_b = copy(has_left, own, head_b, own, right_b, 1, 1, before)
    own_left = copy(has_right, own, tail, own, left, 2, 2, after)
    far_high = copy(above, own, high, far, high, 3, 3, back)
    far_low = copy(above, own, low, far, low, 4, 4, back)
    far_rest = copy(above, own, last_rows, far, last_rows, 6, 14, back)
    far_right_a = copy(both(above, has_right), own, right_a, far, right_a, 5, 5, back)
    far_right_b = copy(both(sec2, has_left), far, head_b, far, right_b, 7, 6, before)
    far_left = copy(both(sec2, has_right), far, tail, far, left, 8, 7, after)
    beside = (True, True, has_right, has_right, has_left, True)

    def hand(condition, source):
        return [
            copy(both(condition, side), source, rows, near, rows, 9 + n, 8 + n, mate)
            for n, (rows, side) in enumerate(zip(pieces, beside))
        ]

    give_own, give_far = hand(odd, own), hand(both(even, sec2), far)
    pair = both(even, sec2)
    near_right_b = copy(both(pair, has_left), far, head_b, near, right_b, 12, 11, (z + 1, s - 1))
    near_left = copy(both(pair, has_right), far, tail, near, left, 13, 12, (z + 1, s + 1))

    def start(what, condition=True):
        @pl.when(both(what[0], condition))
        def _():
            what[1].start()

    def arrive(what, condition):
        @pl.when(condition)
        def _():
            what[1].wait_recv()

    barrier = pltpu.get_barrier_semaphore()
    signals = (
        (both(sec2, no(late)), (z + 2, s)),
        (early, back),
        (has_right, after),
        (has_left, before),
        (takes, mate),
        (both(both(odd, sec1), has_right), (z - 1, s + 1)),
        (both(both(odd, sec1), has_left), (z - 1, s - 1)),
    )
    for condition, where in signals:

        @pl.when(condition)
        def _(where=where):
            pl.semaphore_signal(barrier, inc=1, device_id=where, device_id_type=MESH)

    loads = [
        pltpu.make_async_copy(src, dst, local_sem.at[i])
        for i, (src, dst) in enumerate((
            (image_hbm, own.at[here]), (full_hbm, full_ref), (crop_hbm, crop_out), (off_hbm, off_ref), (flag_hbm, flag_ref)
        ))
    ]
    for load in loads:
        load.start()

    def clear(condition, ref, rows):
        @pl.when(condition)
        def _():
            ref[rows, :] = jnp.zeros((rows.size, P_SIZE), BF16)

    for rows, side in zip(pieces, beside):
        if side is not True:
            clear(no(side), own, rows)
        clear(no(both(sec2, side)), far, rows)
        clear(no(both(takes, side)), near, rows)

    def as_int(condition):
        return condition.astype(jnp.int32)

    expected = as_int(has_left) + as_int(has_right) + as_int(gives)
    expected += as_int(both(above, no(early))) + as_int(late)
    expected += as_int(both(pair, has_left)) + as_int(both(pair, has_right))
    loads[0].wait()
    pl.semaphore_wait(barrier, expected)

    @pl.when(late)
    def _():
        pl.semaphore_signal(ready_sem, inc=1, device_id=(z + 2, s), device_id_type=MESH)

    start(far_high, no(early))
    start(own_right_a)
    start(own_right_b)
    start(far_rest, no(early))
    start(far_low, no(early))
    start(own_left)
    start(give_own[0])
    start(give_own[1])
    start(give_own[5])

    last = both(z == 0, s == 0)

    def pass_strip(condition):
        arrive(far_high, both(condition, sec2))
        for what in (far_right_b, near_right_b, give_far[0]):
            start(what, condition)
        arrive(far_rest, both(condition, sec2))
        for what in (far_left, near_left, give_far[5]):
            start(what, condition)
        arrive(far_low, both(condition, sec2))
        start(give_far[1], condition)

    for load in loads[1:]:
        load.wait()
    rows_to_spectrum_y(own, LOW, y_own, 0, strip, full_ref, strip)
    pass_strip(last)
    arrive(own_right_a, has_right)
    start(far_right_a, no(early))
    start(give_own[2])
    arrive(own_right_b, has_right)
    start(give_own[3])
    arrive(own_left, has_left)
    start(give_own[4])
    rows_to_spectrum_y(own, top, y_own, strip, y_own.shape[1] - strip, full_ref, 224)

    fac_own = []
    for c in range(count):
        spec_own[c], factor = patch_spectrum(y_own, c * STRIDE, full_ref)
        fac_own.append(factor)

    def to_y(which, rows, size):
        rows_to_spectrum_y(part_ref.at[which], rows, y_part.at[which], rows, size, full_ref, 320)

    def spectra(which, patches):
        flag = flag_ref[0, which].astype(F32) * (4.0 / (P_SIZE * P_SIZE * P_SIZE))
        scales = []
        for c in patches:
            start_row = LOW + c * STRIDE + off_ref[which, c]
            spec_part[c], factor = patch_spectrum(y_part.at[which], start_row, full_ref)
            scales.append(jnp.broadcast_to(fac_own[c] * factor * flag, (1, CROP)))
        return scales

    def powers(patches, r_ref):
        for c in patches:
            cross_power(spec_own, spec_part, c, r_ref)

    def partner(which, patches, r_ref):
        scales = spectra(which, patches)
        powers(patches, r_ref)
        return scales

    def windows(patches, scales):
        for c, scale in zip(patches, scales):
            window_ref[c] = crop_window(crop_out, r_first, c, scale)

    def keep(scales):
        for c in range(count):
            scale_second[c : c + 1, :] = scales[c]

    def send_late():
        @pl.when(early)
        def _():
            pl.semaphore_wait(ready_sem, 1)

        for what in (far_high, far_rest, far_low, far_right_a):
            start(what, early)

    def pass_on(condition):
        arrive(far_right_a, both(condition, both(sec2, has_right)))
        start(give_far[2], condition)

    pass_strip(no(last))
    to_y(1, LOW, strip)
    arrive(give_own[0], takes)
    arrive(give_own[1], takes)
    arrive(give_own[5], takes)
    to_y(0, LOW, strip)

    @pl.when(even)
    def _():
        arrive(give_own[2], has_right)
        arrive(give_own[3], has_right)
        arrive(give_own[4], has_left)
        to_y(0, 0, LOW)
        to_y(0, top, HIGH)
        pass_on(last)
        windows(range(count), partner(0, range(count), r_first))
        send_late()
        pass_on(no(last))
        to_y(1, top, HALF)
        arrive(far_right_b, both(sec2, has_right))
        arrive(far_left, both(sec2, has_left))
        to_y(1, 0, LOW)
        to_y(1, top + HALF, HIGH - HALF)
        keep(partner(1, range(count), r_second))

    @pl.when(odd)
    def _():
        arrive(far_right_a, both(sec2, has_right))
        to_y(1, top, HALF)
        windows(INNER, partner(1, INNER, r_first))
        send_late()
        arrive(far_right_b, both(sec2, has_right))
        arrive(far_left, both(sec2, has_left))
        to_y(1, 0, LOW)
        to_y(1, top + HALF, HIGH - HALF)
        outer_scales = partner(1, OUTER, r_first)
        arrive(give_far[2], both(takes, has_right))
        arrive(near_right_b, both(takes, has_right))
        arrive(near_left, both(takes, has_left))
        to_y(0, 0, LOW)
        to_y(0, top, HIGH)
        scales = spectra(0, range(count))
        windows(OUTER, outer_scales)
        powers(range(count), r_second)
        keep(scales)

    sent = [own_right_a, own_right_b, own_left, far_high, far_rest, far_low, far_right_a, far_right_b, far_left]
    for n, far_give in enumerate((*give_far[:3], near_right_b, near_left, give_far[5])):
        sent.append((jnp.logical_or(give_own[n][0], far_give[0]), give_own[n][1]))
    for condition, what in sent:

        @pl.when(condition)
        def _(what=what):
            what.wait_send()


def finish_kernel(window_ref, r_ref, scale_ref, crop_ref, near_hbm, far_hbm, second, sem):
    odd = lax.rem(lax.axis_index("gz"), 2) == 1
    count = window_ref.shape[0]
    group = 2

    def puts(copies):
        @pl.when(odd)
        def _():
            for source, rows, slot in copies:
                first = slot < count // group
                pltpu.make_async_copy(source, (far_hbm if first else near_hbm).at[rows], sem.at[slot]).start()

        @pl.when(jnp.logical_not(odd))
        def _():
            for source, rows, slot in copies:
                first = slot < count // group
                pltpu.make_async_copy(source, (near_hbm if first else far_hbm).at[rows], sem.at[slot]).start()

    rows = [pl.ds(c, group) for c in range(0, count, group)]
    puts([(window_ref.at[r], r, n) for n, r in enumerate(rows)])
    for c in range(count):
        second[c] = crop_window(crop_ref, r_ref, c, scale_ref[c : c + 1, :])
        if c % group == group - 1:
            n = c // group
            puts([(second.at[rows[n]], rows[n], count // group + n)])
    for n, r in enumerate(rows):
        pltpu.make_async_copy(window_ref.at[r], near_hbm.at[r], sem.at[n]).wait()
        pltpu.make_async_copy(second.at[r], near_hbm.at[r], sem.at[count // group + n]).wait()


def solution(mesh):
    depth, width = mesh.shape["gz"], mesh.shape["gx"]
    full, crop = transform_tables()

    def on_device(image, flags, offsets):
        count = offsets.shape[2]
        strip = image.shape[2]
        total = LOW + strip + HIGH
        vmem = pl.BlockSpec(memory_space=pltpu.VMEM)
        hbm = pl.BlockSpec(memory_space=pltpu.HBM)
        window = jax.ShapeDtypeStruct((count, CROP, CROP), F32)
        spectra = jax.ShapeDtypeStruct((count, P_SIZE, P_SIZE), BF16)
        scale = jax.ShapeDtypeStruct((count, CROP), F32)

        def body(*refs):
            exchange_kernel(depth, width, *refs)

        first, cross, scales, table = pl.pallas_call(
            body,
            out_shape=[window, spectra, scale, jax.ShapeDtypeStruct((CROP, P_SIZE), BF16)],
            in_specs=[hbm] * 5,
            out_specs=[vmem] * 4,
            scratch_shapes=[
                pltpu.VMEM((total, P_SIZE), BF16),
                pltpu.VMEM((2, total, P_SIZE), BF16),
                pltpu.VMEM((2, 544, HALF), F32),
                pltpu.VMEM((2, 2, total, HALF), F32),
                pltpu.VMEM((count, P_SIZE, P_SIZE), F32),
                pltpu.VMEM((count, P_SIZE, P_SIZE), F32),
                pltpu.VMEM((count, P_SIZE, P_SIZE), BF16),
                pltpu.VMEM((P_SIZE, P_SIZE), BF16),
                pltpu.SMEM((2, count), jnp.int32),
                pltpu.SMEM((1, 2), jnp.int32),
                pltpu.SemaphoreType.DMA((15,)),
                pltpu.SemaphoreType.DMA((15,)),
                pltpu.SemaphoreType.DMA((5,)),
                pltpu.SemaphoreType.REGULAR,
            ],
            name="exchange",
            compiler_params=pltpu.CompilerParams(
                collective_id=0, has_side_effects=True, vmem_limit_bytes=40 * 2**20
            ),
        )(*(
            pltpu.with_memory_space_constraint(operand, pltpu.HBM)
            for operand in (
                jnp.transpose(offsets[0, 0]), flags, jnp.transpose(image[0]), jnp.asarray(full), jnp.asarray(crop)
            )
        ))
        near, far = pl.pallas_call(
            finish_kernel,
            out_shape=[window, window],
            in_specs=[vmem] * 4,
            out_specs=[hbm] * 2,
            scratch_shapes=[
                pltpu.VMEM((count, CROP, CROP), F32),
                pltpu.SemaphoreType.DMA((count,)),
            ],
            name="finish",
            compiler_params=pltpu.CompilerParams(vmem_limit_bytes=16 * 2**20),
        )(first, cross, scales, table)
        shape = (1, 1, count, CROP, CROP)
        return near.reshape(shape), far.reshape(shape)

    in_specs = (P("gz", None, "gx"), P("gz", None), P("gz", None, "gx", None))
    out_specs = (P("gz", None, "gx", None, None), P("gz", None, "gx", None, None))
    return jax.shard_map(
        on_device, mesh=mesh, in_specs=in_specs, out_specs=out_specs, check_vma=False
    )
```
